256 devices in a mesh: seq: 64 (over y, z_hi, x), tp: 4 (over z_lo, core).
Axes of the slice: x: 4, y: 4, z: 8 (z_hi: 4, z_lo: 2; z = z_hi * 2 + z_lo), core: 2. Of those that a mesh axis runs over, the one named last changes fastest.
Arguments:
- tokens: bfloat16 [32256, 4096], P('seq'), may hold values from -6 to 6
- norm_gain: float32 [4096], replicated, may hold values from 0.5 to 1.5
- gate_weight: bfloat16 [4096, 7168], P('seq', 'tp'), may hold values from -0.09375 to 0.09375
- up_weight: bfloat16 [4096, 7168], P('seq', 'tp'), may hold values from -0.09375 to 0.09375
Outputs:
- saved_hidden: bfloat16 [32256, 7168], P('seq', 'tp')
- token_scales: float32 [32256], P('seq')
The draws below stay inside these ranges and needn't reach their ends.
All inputs are finite; a program needn't handle non-finite values. Where the reference program divides by a largest or mean magnitude, that divisor is 1e-20 or more.
Results may differ from the reference program's by a relative error of at most 0.0061.
Values may be sent and summed in bfloat16 or wider, within the bound.
A program may use at most 128 MiB of HBM per device.

```python
import jax
import jax.numpy as jnp
from jax import lax

D = 4096
FF = 7168
TOK_DEV = 504
TOKENS = 32256
N_SEQ = 64


def shard_levels(stream_key, extent, shards, low, high):
    gain, own = 1.0, jax.random.fold_in(stream_key, 6)
    for dim, parts in shards:
        draws = jnp.exp(jax.random.uniform(jax.random.fold_in(own, dim), (parts,), jnp.float32, low / len(shards), high / len(shards)))
        gain = gain * jnp.repeat(draws, extent[dim] // parts).reshape([-1 if axis == dim else 1 for axis in range(len(extent))])
    return gain


def normal_values(stream_key, dims, scale, limit, pieces=(), kind=jnp.bfloat16):
    level = shard_levels(stream_key, dims, pieces, -0.22, 0.18) if pieces else 1.0
    result = jax.random.normal(stream_key, dims, jnp.float32) * scale * level
    return jnp.minimum(jnp.maximum(result, -limit), limit).astype(kind)


def setup_inputs(seed: int = 0) -> dict:
    streams_of = jax.random.split(jax.random.key(seed), 5)
    tokens = normal_values(streams_of[0], (TOKENS, D), 1.0, 6.0, ((0, 64),))
    norm_gain = jnp.clip(1.0 + 0.1 * jax.random.normal(streams_of[1], (D,), jnp.float32), 0.5, 1.5)
    gate_weight = normal_values(streams_of[2], (D, FF), D ** -0.5, 0.09375, ((0, 64), (1, 4)))
    up_weight = normal_values(streams_of[3], (D, FF), D ** -0.5, 0.09375, ((0, 64), (1, 4)))
    return dict(tokens=tokens, norm_gain=norm_gain, gate_weight=gate_weight, up_weight=up_weight)


def norm_rows(block, norm_gain):
    values = block.astype(jnp.float32)
    mean_square = lax.optimization_barrier(jnp.mean(values * values, axis=1, keepdims=True))
    return (values * lax.rsqrt(mean_square + 1e-05) * norm_gain[None, :]).astype(jnp.bfloat16)

def reference(tokens, norm_gain, gate_weight, up_weight):
    blocks = tokens.reshape(N_SEQ, TOK_DEV, D)

    def one_block(block):
        normed = norm_rows(block, norm_gain)
        gate = jnp.dot(normed, gate_weight, preferred_element_type=jnp.float32)
        up = jnp.dot(normed, up_weight, preferred_element_type=jnp.float32)
        hidden = jax.nn.silu(gate) * up
        scales = lax.optimization_barrier(jnp.max(jnp.abs(hidden), axis=1)) + 1e-06
        saved = (hidden / scales[:, None]).astype(jnp.bfloat16)
        return (saved, scales)
    saved, scales = lax.map(one_block, blocks)
    return (saved.reshape(TOKENS, FF), scales.reshape(TOKENS))
```

```python
import functools

import jax
import jax.numpy as jnp
from jax import lax
from jax.experimental import pallas as pl
from jax.experimental.pallas import tpu as pltpu
from jax.sharding import PartitionSpec as P

MESH = pl.DeviceIdType.MESH
TOK = 504
PAD = 512
D = 4096
PIECE = 896
NCOL = 2 * PIECE
ROWS = 128
EPS = 1e-05


def mod(v, n):
    return lax.rem(v + 2 * n, n)


def kernel(tok_hbm, gain_ref, gate_hbm, up_hbm, out_ref, scale_ref,
           raw, tok, w, acc, osend, orecv, psend, precv,
           raw_sem, s1_ss, s1_rs, t_ss, t_rs, r_ss, r_rs, z_ss, z_rs, y_ss, y_rs,
           b_ss, b_rs, o_ss, o_rs, p_ss, p_rs):
    s = lax.axis_index("seq")
    t = lax.axis_index("tp")
    x = s % 4
    zh = (s // 4) % 4
    y = s // 16
    zl = t // 2
    c = t % 2

    def dev(xx, yy, zz, ll, cc):
        return ((yy * 4 + zz) * 4 + xx, ll * 2 + cc)

    def rc(src, dst, ssem, rsem, target):
        return pltpu.make_async_remote_copy(
            src_ref=src, dst_ref=dst, send_sem=ssem, recv_sem=rsem,
            device_id=target, device_id_type=MESH)

    xp, xm = mod(x + 1, 4), mod(x - 1, 4)
    yp, ym = mod(y + 1, 4), mod(y - 1, 4)
    zp, zm = mod(zh + 1, 4), mod(zh - 1, 4)
    sib = dev(x, y, zh, zl, 1 - c)
    y_up, y_dn = dev(x, yp, zh, zl, c), dev(x, ym, zh, zl, c)
    z_up, z_dn = dev(x, y, zp, zl, c), dev(x, y, zm, zl, c)

    raw_copy = pltpu.make_async_copy(tok_hbm, raw, raw_sem)
    raw_copy.start()

    barrier = pltpu.get_barrier_semaphore()
    for dx in range(4):
        for ll in range(2):
            for cc in range(2):
                if dx == 0 and ll == 0 and cc == 0:
                    continue
                pl.semaphore_signal(
                    barrier, inc=1, device_id_type=MESH,
                    device_id=dev(mod(x + dx, 4), y, zh, (zl + ll) % 2, (c + cc) % 2))
    for target in (y_up, y_dn, z_up, z_dn):
        pl.semaphore_signal(barrier, inc=1, device_id=target, device_id_type=MESH)
    pl.semaphore_wait(barrier, 19)

    def base(zz, yy):
        return pl.multiple_of((zz * 4 + yy) * 256, 256)

    def w_part(r, n):
        return w.at[pl.ds(pl.multiple_of(r, 64), n)]

    def s1_dst(xx, g):
        return w.at[pl.ds(pl.multiple_of(base(zh, y) + xx * 64, 64), 64), pl.ds(g * PIECE, PIECE)]

    def s1_copy(h, g):
        src = (gate_hbm, up_hbm)[g].at[:, pl.ds(h * PIECE, PIECE)]
        sem = s1_rs.at[(x % 2) * 2 + g]
        return src, s1_dst(x, g), sem

    for h in range(2):
        mine = jnp.logical_and(x // 2 == c, x % 2 == h)
        for g in range(2):
            src, dst, sem = s1_copy(h, g)

            @pl.when(mine)
            def _():
                pltpu.make_async_copy(src, dst, sem).start()

            @pl.when(jnp.logical_not(mine))
            def _():
                rc(src, dst, s1_ss.at[h * 2 + g], sem, dev(2 * c + h, y, zh, zl, x // 2)).start()

    raw_copy.wait()
    gain = gain_ref[...].reshape(1, D)

    def normed(values):
        v = values.astype(jnp.float32)
        mean_square = jnp.sum(v * v, axis=1, keepdims=True) * (1.0 / D)
        return (v * lax.rsqrt(mean_square + EPS) * gain).astype(jnp.bfloat16)

    def put(r, n, val):
        for yy in range(4):
            for zz in range(4):
                a, b = (yy * 4 + zz) * 256, (zz * 4 + yy) * 256
                tok[2, pl.ds(r, n), pl.ds(b, 256)] = val[:, a:a + 256]

    def norm_group(i, carry):
        r = pl.multiple_of(i * 16, 16)
        put(r, 16, normed(raw[pl.ds(r, 16), :]))
        return carry

    def tok_chunk(slot, j):
        return tok.at[slot, pl.ds(j * ROWS, ROWS)]

    t_target = dev(mod(x + 1 - 2 * c, 4), y, zh, zl, 1)

    def t_send(j):
        return rc(tok_chunk(2, j), tok_chunk(c, j), t_ss.at[j], t_rs.at[c * 4 + j], t_target)

    for j in range(4):
        lax.fori_loop(j * 8, j * 8 + (7 if j == 3 else 8), norm_group, 0)
        if j == 3:
            tail = normed(raw[pl.ds(496, 8), :])
            put(496, 16, jnp.concatenate([tail, jnp.zeros((8, D), jnp.bfloat16)], axis=0))
        t_send(j).start()

    def chunk(zz, yy, cc):
        return w_part(base(zz, yy) + cc * 128, 128)

    def half(zz, yy, hh):
        return w_part(base(zz, yy) + c * 128 + hh * 64, 64)

    rels = (0, 1, 3, 2)
    zz_of = {r: mod(zh + r, 4) for r in rels}
    yy_of = {0: y, 1: yp, 3: ym, 2: mod(y + 2, 4)}

    def b_copy(r, q):
        ref = chunk(zz_of[r], yy_of[q], c)
        return rc(ref, ref, b_ss.at[r * 4 + q], b_rs.at[r * 4 + q], sib)

    def b_wait(r):
        for q in range(4):
            ref = chunk(zz_of[r], yy_of[q], 1 - c)
            rc(ref, ref, b_ss.at[r * 4 + q], b_rs.at[r * 4 + q], sib).wait_recv()

    def y_send(r, d):
        ref = chunk(zz_of[r], y, c)
        return rc(ref, ref, y_ss.at[r * 4 + d], y_rs.at[r * 4 + d], (y_up, y_dn)[d])

    def y_relay(r, d):
        ref = half(zz_of[r], (ym, yp)[d], d)
        return rc(ref, ref, y_ss.at[r * 4 + 2 + d], y_rs.at[r * 4 + 2 + d], (y_up, y_dn)[d])

    def y_arrived(r, d):
        ref = chunk(zz_of[r], (ym, yp)[d], c)
        rc(ref, ref, y_ss.at[r * 4 + d], y_rs.at[r * 4 + d], sib).wait_recv()

    def y_opposite(r):
        for d in range(2):
            ref = half(zz_of[r], yy_of[2], d)
            rc(ref, ref, y_ss.at[r * 4 + 2 + d], y_rs.at[r * 4 + 2 + d], sib).wait_recv()

    def z_send(d):
        ref = chunk(zh, y, c)
        return rc(ref, ref, z_ss.at[d], z_rs.at[d], (z_up, z_dn)[d])

    def z_relay(d):
        ref = half((zm, zp)[d], y, d)
        return rc(ref, ref, z_ss.at[2 + d], z_rs.at[2 + d], (z_up, z_dn)[d])

    def z_arrived(d):
        ref = chunk((zm, zp)[d], y, c)
        rc(ref, ref, z_ss.at[d], z_rs.at[d], sib).wait_recv()

    def z_opposite():
        for d in range(2):
            ref = half(zz_of[2], y, d)
            rc(ref, ref, z_ss.at[2 + d], z_rs.at[2 + d], sib).wait_recv()

    def y_step(r):
        for d in range(2):
            y_arrived(r, d)
            y_relay(r, d).start()
        b_copy(r, 3).start()
        b_copy(r, 1).start()

    def y_finish(r):
        y_opposite(r)
        b_copy(r, 2).start()
        b_wait(r)

    def t_arrived(j):
        for slot in range(2):
            ref = tok_chunk(slot, j)
            rc(ref, ref, t_ss.at[j], t_rs.at[slot * 4 + j], sib).wait_recv()

    def relay(j):
        slot = j % 2
        target = dev((xp, xm)[slot], y, zh, zl, 0)
        return rc(tok_chunk(slot, j), tok_chunk(1, j), r_ss.at[j], r_rs.at[j], target)

    def t_step(j):
        @pl.when(c == 1)
        def _():
            t_arrived(j)
            relay(j).start()

    def opp_arrived(j):
        ref = tok_chunk(1, j)
        rc(ref, ref, r_ss.at[j], r_rs.at[j], sib).wait_recv()

    first = jnp.where(c == 0, 2, 0)

    def unit(slot, r, r0=0, nr=PAD, start=False):
        src = first if slot == 0 else 1
        k0 = pl.multiple_of(zz_of[r] * 1024, 1024)

        def col(n, carry):
            cols = pl.ds(pl.multiple_of(n * 256, 256), 256)
            part = jnp.dot(tok[src, pl.ds(r0, nr), pl.ds(k0, 1024)], w[pl.ds(k0, 1024), cols],
                           preferred_element_type=jnp.float32)
            if start:
                acc[slot, pl.ds(r0, nr), cols] = part
            else:
                acc[slot, pl.ds(r0, nr), cols] += part
            return carry

        lax.fori_loop(0, NCOL // 256, col, 0)

    for p in range(2):
        for g in range(2):
            ref = s1_dst(2 * c + p, g)
            rc(ref, ref, s1_ss.at[0], s1_rs.at[p * 2 + g], sib).wait_recv()
    for d in range(2):
        y_send(0, d).start()
        z_send(d).start()
    b_copy(0, 0).start()

    t_step(0)
    y_step(0)
    t_step(1)
    for d, r in ((0, 3), (1, 1)):
        z_arrived(d)
        z_relay(d).start()
        b_copy(r, 0).start()
    for r in (1, 3):
        y_send(r, 0).start()
        y_send(r, 1).start()
    y_finish(0)

    @pl.when(c == 0)
    def _():
        unit(0, 0, start=True)

    z_opposite()
    y_send(2, 0).start()
    y_send(2, 1).start()
    b_copy(2, 0).start()
    t_step(2)
    y_step(1)
    t_step(3)

    @pl.when(c == 1)
    def _():
        unit(0, 0, start=True)
        unit(1, 0, start=True)

    y_finish(1)
    unit(0, 1)

    @pl.when(c == 1)
    def _():
        unit(1, 1)

    y_step(3)
    y_finish(3)
    unit(0, 3)

    @pl.when(c == 1)
    def _():
        unit(1, 3)

    y_step(2)

    @pl.when(c == 0)
    def _():
        for j0 in (0, 2):
            opp_arrived(j0)
            opp_arrived(j0 + 1)
            unit(1, 0, j0 * ROWS, 256, start=True)
            unit(1, 1, j0 * ROWS, 256)
            unit(1, 3, j0 * ROWS, 256)

    y_finish(2)

    def hidden(slot):
        def rows(i, carry):
            r = pl.ds(pl.multiple_of(i * ROWS, ROWS), ROWS)
            peak = jnp.zeros((ROWS, 128), jnp.float32)
            for n in range(PIECE // 128):
                gate = acc[slot, r, pl.ds(n * 128, 128)]
                up = acc[slot, r, pl.ds(PIECE + n * 128, 128)]
                val = gate / (1.0 + jnp.exp(-gate)) * up
                peak = jnp.maximum(peak, jnp.abs(val))
                osend[slot, r, pl.ds(n * 128, 128)] = val.astype(jnp.bfloat16)
            top = jnp.max(peak.T, axis=0, keepdims=True)
            psend[slot, :, r] = jnp.broadcast_to(top, (8, ROWS))
            return carry

        lax.fori_loop(0, PAD // ROWS, rows, 0)

    rel_of = (jnp.where(c == 0, 0, 3), jnp.where(c == 0, 2, 1))

    def to_owner(slot, wait):
        rel = rel_of[slot]
        xb = mod(x + rel, 4)

        def move(src, dst, ssem, rsem, ll, cc):
            here = jnp.logical_and(rel == 0, jnp.logical_and(ll == zl, cc == c))

            @pl.when(jnp.logical_not(here))
            def _():
                copy = rc(src, dst, ssem, rsem, dev(xb, y, zh, ll, cc))
                if wait:
                    copy.wait_send()
                else:
                    copy.start()

            if not wait:
                @pl.when(here)
                def _():
                    pltpu.make_async_copy(src, dst, rsem).start()

        index = rel * 2 + zl
        for k in range(4):
            move(psend.at[slot], precv.at[index], p_ss.at[slot * 4 + k], p_rs.at[index], k // 2, k % 2)
        move(osend.at[slot], orecv.at[:, pl.ds(pl.multiple_of((x % 2) * PIECE, 128), PIECE)],
             o_ss.at[slot], o_rs.at[x % 2], zl, x // 2)

    unit(0, 2)
    hidden(0)
    to_owner(0, False)

    @pl.when(c == 1)
    def _():
        unit(1, 2)

    @pl.when(c == 0)
    def _():
        unit(1, 2)

    hidden(1)
    to_owner(1, False)

    top = None
    for i in range(8):
        ref = precv.at[i]
        rc(ref, ref, p_ss.at[0], p_rs.at[i], sib).wait_recv()
    top = precv[0]
    for i in range(1, 8):
        top = jnp.maximum(top, precv[i])
    top = top + 1e-06
    scale_ref[...] = top[0, :TOK]
    psend_inv = 1.0 / top
    for p in range(2):
        ref = orecv.at[:, pl.ds(p * PIECE, PIECE)]
        rc(ref, ref, o_ss.at[0], o_rs.at[p], sib).wait_recv()
    for i in range(PAD // ROWS):
        n = min(ROWS, TOK - i * ROWS)
        inv = jnp.broadcast_to(psend_inv[:1, i * ROWS:(i + 1) * ROWS], (ROWS, ROWS)).T
        for k in range(NCOL // 128):
            val = orecv[pl.ds(i * ROWS, ROWS), pl.ds(k * 128, 128)].astype(jnp.float32) * inv
            out_ref[pl.ds(i * ROWS, n), pl.ds(k * 128, 128)] = val.astype(jnp.bfloat16)[:n]

    for h in range(2):
        mine = jnp.logical_and(x // 2 == c, x % 2 == h)
        for g in range(2):
            src, dst, sem = s1_copy(h, g)

            @pl.when(jnp.logical_not(mine))
            def _():
                rc(src, dst, s1_ss.at[h * 2 + g], sem, sib).wait_send()
    for j in range(4):
        t_send(j).wait_send()

        @pl.when(c == 1)
        def _():
            relay(j).wait_send()
    for d in range(2):
        z_send(d).wait_send()
        z_relay(d).wait_send()
        for r in rels:
            y_send(r, d).wait_send()
            y_relay(r, d).wait_send()
    for r in rels:
        for q in range(4):
            b_copy(r, q).wait_send()
    to_owner(0, True)
    to_owner(1, True)


def shards(tokens, norm_gain, gate_weight, up_weight):
    dma = pltpu.SemaphoreType.DMA
    vmem = pl.BlockSpec(memory_space=pltpu.VMEM)
    hbm = pl.BlockSpec(memory_space=pl.ANY)
    return pl.pallas_call(
        kernel,
        name="block",
        out_shape=(jax.ShapeDtypeStruct((TOK, NCOL), jnp.bfloat16),
                   jax.ShapeDtypeStruct((TOK,), jnp.float32)),
        in_specs=[hbm, vmem, hbm, hbm],
        out_specs=(vmem, vmem),
        scratch_shapes=[
            pltpu.VMEM((TOK, D), jnp.bfloat16),
            pltpu.VMEM((3, PAD, D), jnp.bfloat16),
            pltpu.VMEM((D, NCOL), jnp.bfloat16),
            pltpu.VMEM((2, PAD, NCOL), jnp.float32),
            pltpu.VMEM((2, PAD, PIECE), jnp.bfloat16),
            pltpu.VMEM((PAD, NCOL), jnp.bfloat16),
            pltpu.VMEM((2, 8, PAD), jnp.float32),
            pltpu.VMEM((8, 8, PAD), jnp.float32),
            dma, dma((4,)), dma((4,)), dma((4,)), dma((8,)), dma((4,)), dma((4,)),
            dma((4,)), dma((4,)), dma((16,)), dma((16,)), dma((16,)), dma((16,)),
            dma((2,)), dma((2,)), dma((8,)), dma((8,)),
        ],
        compiler_params=pltpu.CompilerParams(
            collective_id=0, has_side_effects=True, vmem_limit_bytes=58 * 2**20),
    )(tokens, norm_gain, gate_weight, up_weight)


def solution(mesh):
    in_specs = (P("seq", None), P(), P("seq", "tp"), P("seq", "tp"))
    out_specs = (P("seq", "tp"), P("seq"))
    return jax.shard_map(shards, mesh=mesh, in_specs=in_specs, out_specs=out_specs, check_vma=False)
```

```python
import jax
import jax.numpy as jnp
from jax import lax
from jax.experimental import pallas as pl
from jax.experimental.pallas import tpu as pltpu
from jax.sharding import PartitionSpec as P

MESH = pl.DeviceIdType.MESH
TOK = 504
PAD = 512
D = 4096
PIECE = 896
NCOL = 2 * PIECE
ROWS = 128
EPS = 1e-05
WIDTH = (256, 256, 256, 128)
START = (0, 256, 512, 768)
G = len(WIDTH)
ND, NQ = 1, 2


def mod(v, n):
    return lax.rem(v + 2 * n, n)


def kernel(tok_hbm, gain_ref, gate_hbm, up_hbm, out_ref, scale_ref,
           raw, tok, *rest):
    w = rest[:G]
    (peak, osend, orecv, psend, precv, raw_sem, s1_ss, s1_rs, t_ss, t_rs, f_ss, r_ss, r_rs, q_ss,
     z_ss, z_rs, y_ss, y_rs, b_ss, b_rs, o_ss, o_rs, p_ss, p_rs) = rest[G:]
    s = lax.axis_index("seq")
    t = lax.axis_index("tp")
    x = s % 4
    zh = (s // 4) % 4
    y = s // 16
    zl = t // 2
    c = t % 2

    def dev(xx, yy, zz, ll, cc):
        return ((yy * 4 + zz) * 4 + xx, ll * 2 + cc)

    def rc(src, dst, ssem, rsem, target):
        return pltpu.make_async_remote_copy(
            src_ref=src, dst_ref=dst, send_sem=ssem, recv_sem=rsem,
            device_id=target, device_id_type=MESH)

    xp, xm = mod(x + 1, 4), mod(x - 1, 4)
    yp, ym = mod(y + 1, 4), mod(y - 1, 4)
    zp, zm = mod(zh + 1, 4), mod(zh - 1, 4)
    sib = dev(x, y, zh, zl, 1 - c)
    pair = dev(x, y, zh, 1 - zl, c)
    y_up, y_dn = dev(x, yp, zh, zl, c), dev(x, ym, zh, zl, c)
    z_up, z_dn = dev(x, y, zp, zl, c), dev(x, y, zm, zl, c)

    raw_copy = pltpu.make_async_copy(tok_hbm, raw, raw_sem)
    raw_copy.start()

    barrier = pltpu.get_barrier_semaphore()
    for dx in range(4):
        for ll in range(2):
            for cc in range(2):
                if dx == 0 and ll == 0 and cc == 0:
                    continue
                pl.semaphore_signal(
                    barrier, inc=1, device_id_type=MESH,
                    device_id=dev(mod(x + dx, 4), y, zh, (zl + ll) % 2, (c + cc) % 2))
    for target in (y_up, y_dn, z_up, z_dn):
        pl.semaphore_signal(barrier, inc=1, device_id=target, device_id_type=MESH)

    raw_copy.wait()
    gain = gain_ref[...].reshape(1, D)

    def normed(values):
        v = values.astype(jnp.float32)
        mean_square = jnp.sum(v * v, axis=1, keepdims=True) * (1.0 / D)
        return (v * lax.rsqrt(mean_square + EPS) * gain).astype(jnp.bfloat16)

    def put(r, n, val):
        for yy in range(4):
            for zz in range(4):
                a, b = (yy * 4 + zz) * 256, (zz * 4 + yy) * 256
                tok[2, pl.ds(r, n), pl.ds(b, 256)] = val[:, a:a + 256]

    def norm_group(i, carry):
        r = pl.multiple_of(i * 16, 16)
        put(r, 16, normed(raw[pl.ds(r, 16), :]))
        return carry

    lax.fori_loop(0, 31, norm_group, 0)
    tail = normed(raw[pl.ds(496, 8), :])
    put(496, 16, jnp.concatenate([tail, jnp.zeros((8, D), jnp.bfloat16)], axis=0))
    peak[...] = jnp.zeros_like(peak)

    pl.semaphore_wait(barrier, 19)

    def chunk(g, zz, yy, cc):
        return w[g].at[zz * 4 + yy, cc]

    def half(g, zz, yy, hh):
        return w[g].at[zz * 4 + yy, c, pl.ds(hh * 64, 64)]

    def s1_dst(g, xx, u):
        return w[g].at[zh * 4 + y, xx // 2, pl.ds(pl.multiple_of((xx % 2) * 64, 64), 64),
                       pl.ds(u * WIDTH[g], WIDTH[g])]

    def s1_copy(g, h, u):
        src = (gate_hbm, up_hbm)[u].at[:, pl.ds(h * PIECE + START[g], WIDTH[g])]
        return src, s1_dst(g, x, u), s1_rs.at[g * 4 + (x % 2) * 2 + u]

    def s1_each(act):
        for g in range(G):
            for h in range(2):
                mine = jnp.logical_and(x // 2 == c, x % 2 == h)
                for u in range(2):
                    act(g, h, u, mine)

    def s1_start(g, h, u, mine):
        src, dst, sem = s1_copy(g, h, u)

        @pl.when(mine)
        def _():
            pltpu.make_async_copy(src, dst, sem).start()

        @pl.when(jnp.logical_not(mine))
        def _():
            rc(src, dst, s1_ss.at[g * 4 + h * 2 + u], sem, dev(2 * c + h, y, zh, zl, x // 2)).start()

    def s1_sent(g, h, u, mine):
        src, dst, sem = s1_copy(g, h, u)

        @pl.when(jnp.logical_not(mine))
        def _():
            rc(src, dst, s1_ss.at[g * 4 + h * 2 + u], sem, sib).wait_send()

    s1_each(s1_start)

    def tok_half(slot, q):
        return tok.at[slot, pl.ds(pl.multiple_of(jnp.where(zl == 0, q, 7 - q) * 64, 64), 64)]

    t_target = dev(mod(x + 1 - 2 * c, 4), y, zh, zl, 1)

    def t_send(q):
        return rc(tok_half(2, q), tok_half(c, q), t_ss.at[q], t_rs.at[c * 8 + q], t_target)

    for q in range(8 - ND):
        t_send(q).start()

    def t_arrived(slot, q):
        ref = tok_half(slot, q)
        rc(ref, ref, t_ss.at[0], t_rs.at[slot * 8 + q], sib).wait_recv()

    def t_copy(slot, q):
        ref = tok_half(slot, q)
        return rc(ref, ref, f_ss.at[slot * 2 + q], t_rs.at[slot * 8 + 7 - q], pair)

    def relay(q):
        slot = q % 2
        target = dev((xp, xm)[slot], y, zh, zl, 0)
        return rc(tok_half(slot, q), tok_half(1, q), r_ss.at[q], r_rs.at[q], target)

    def opp_arrived(q):
        ref = tok_half(1, q)
        rc(ref, ref, r_ss.at[0], r_rs.at[q], sib).wait_recv()

    def opp_copy(q):
        ref = tok_half(1, q)
        return rc(ref, ref, q_ss.at[q], r_rs.at[7 - q], pair)

    def t_step(q):
        @pl.when(c == 1)
        def _():
            for slot in range(2):
                t_arrived(slot, q)
            if q < 8 - NQ:
                relay(q).start()

    def t_pass(slot, q):
        @pl.when(c == 1)
        def _():
            t_copy(slot, q).start()

    def t_last():
        @pl.when(c == 1)
        def _():
            for slot in range(2):
                for q in range(8 - ND, 8):
                    t_arrived(slot, q)

    def q_pass(q):
        @pl.when(c == 0)
        def _():
            opp_arrived(q)
            opp_copy(q).start()

    def q_last():
        @pl.when(c == 0)
        def _():
            for q in range(NQ, 8):
                opp_arrived(q)

    rels = (0, 1, 3, 2)
    zz_of = {r: mod(zh + r, 4) for r in rels}
    yy_of = {0: y, 1: yp, 3: ym, 2: mod(y + 2, 4)}

    def b_copy(g, r, cc):
        ref = w[g].at[pl.ds(pl.multiple_of(zz_of[r] * 4, 4), 4), cc]
        return rc(ref, ref, b_ss.at[g * 4 + r], b_rs.at[g * 4 + r], sib)

    def b_wait(g):
        for r in rels:
            b_copy(g, r, 1 - c).wait_recv()

    def y_copy(g, r, d):
        ref = chunk(g, zz_of[r], y, c)
        i = (g * 4 + r) * 4 + d
        return rc(ref, ref, y_ss.at[i], y_rs.at[i], (y_up, y_dn)[d])

    def y_relay(g, r, d):
        ref = half(g, zz_of[r], (ym, yp)[d], d)
        i = (g * 4 + r) * 4 + 2 + d
        return rc(ref, ref, y_ss.at[i], y_rs.at[i], (y_up, y_dn)[d])

    def z_copy(g, d):
        ref = chunk(g, zh, y, c)
        return rc(ref, ref, z_ss.at[g * 4 + d], z_rs.at[g * 4 + d], (z_up, z_dn)[d])

    def z_relay(g, d):
        ref = half(g, (zm, zp)[d], y, d)
        return rc(ref, ref, z_ss.at[g * 4 + 2 + d], z_rs.at[g * 4 + 2 + d], (z_up, z_dn)[d])

    def own(g):
        for p in range(2):
            for u in range(2):
                ref = s1_dst(g, 2 * c + p, u)
                rc(ref, ref, s1_ss.at[0], s1_rs.at[g * 4 + p * 2 + u], sib).wait_recv()

    def z_send(g):
        for d in range(2):
            z_copy(g, d).start()

    def z_near(g):
        for d in range(2):
            ref = chunk(g, (zm, zp)[d], y, c)
            rc(ref, ref, z_ss.at[0], z_rs.at[g * 4 + d], sib).wait_recv()
            z_relay(g, d).start()

    def z_far(g):
        for d in range(2):
            ref = half(g, zz_of[2], y, d)
            rc(ref, ref, z_ss.at[0], z_rs.at[g * 4 + 2 + d], sib).wait_recv()

    def y_send(g, r):
        for d in range(2):
            y_copy(g, r, d).start()

    def y_near(g, r):
        for d in range(2):
            ref = chunk(g, zz_of[r], (ym, yp)[d], c)
            rc(ref, ref, y_ss.at[0], y_rs.at[(g * 4 + r) * 4 + d], sib).wait_recv()
            y_relay(g, r, d).start()

    def y_far(g, r):
        for d in range(2):
            ref = half(g, zz_of[r], yy_of[2], d)
            rc(ref, ref, y_ss.at[0], y_rs.at[(g * 4 + r) * 4 + 2 + d], sib).wait_recv()
        b_copy(g, r, c).start()

    first = jnp.where(c == 0, 2, 0)
    rel_of = (jnp.where(c == 0, 0, 3), jnp.where(c == 0, 2, 1))

    def move(rel, src, dst, ssem, rsem, ll, cc, wait):
        here = jnp.logical_and(rel == 0, jnp.logical_and(ll == zl, cc == c))

        @pl.when(jnp.logical_not(here))
        def _():
            copy = rc(src, dst, ssem, rsem, dev(mod(x + rel, 4), y, zh, ll, cc))
            if wait:
                copy.wait_send()
            else:
                copy.start()

        if not wait:
            @pl.when(here)
            def _():
                pltpu.make_async_copy(src, dst, rsem).start()

    def out_move(slot, g, wait=False):
        n = WIDTH[g]
        dst = orecv.at[:, pl.ds(pl.multiple_of((x % 2) * PIECE + START[g], 128), n)]
        move(rel_of[slot], osend.at[slot, :, pl.ds(START[g], n)], dst,
             o_ss.at[slot * G + g], o_rs.at[(x % 2) * G + g], zl, x // 2, wait)

    def peak_move(slot, wait=False):
        index = rel_of[slot] * 2 + zl
        for k in range(4):
            move(rel_of[slot], psend.at[slot], precv.at[index],
                 p_ss.at[slot * 4 + k], p_rs.at[index], k // 2, k % 2, wait)

    def unit(slot, g):
        n = WIDTH[g]
        src = first if slot == 0 else 1
        res = jnp.dot(tok[src], w[g][...].reshape(D, 2 * n), preferred_element_type=jnp.float32)
        gate, up = res[:, :n], res[:, n:]
        val = gate / (1.0 + jnp.exp(-gate)) * up
        top = peak[slot]
        for k in range(0, n, 128):
            top = jnp.maximum(top, jnp.abs(val[:, k:k + 128]))
        peak[slot] = top
        osend[slot, :, pl.ds(START[g], n)] = val.astype(jnp.bfloat16)
        if g < G - 1:
            out_move(slot, g)

    def on(core, *calls):
        @pl.when(c == core)
        def _():
            for slot, g in calls:
                unit(slot, g)

    def peak_out(slot):
        for i in range(4):
            r = pl.ds(i * 128, 128)
            top = jnp.max(peak[slot, r].T, axis=0, keepdims=True)
            psend[slot, :, r] = jnp.broadcast_to(top, (8, 128))
        peak_move(slot)

    own(0)
    y_send(0, 0)
    z_send(0)
    own(1)
    y_send(1, 0)
    own(2)
    y_send(2, 0)
    own(3)
    y_send(3, 0)
    y_near(0, 0)
    y_near(1, 0)
    z_near(0)
    z_send(1)
    y_send(0, 1)
    y_send(0, 3)
    t_step(0)
    t_pass(0, 0)
    t_pass(1, 0)
    y_near(2, 0)
    y_near(3, 0)
    y_far(0, 0)
    z_near(1)
    y_send(1, 1)
    t_step(1)
    y_send(1, 3)
    z_far(0)
    y_send(0, 2)
    y_far(1, 0)
    y_near(0, 1)
    y_near(0, 3)
    t_step(2)
    y_far(2, 0)
    t_step(3)
    y_far(3, 0)
    y_near(1, 1)
    y_near(1, 3)
    z_far(1)
    z_send(2)
    y_send(1, 2)
    t_step(4)
    y_near(0, 2)
    y_far(0, 1)
    y_far(0, 3)
    z_send(3)
    y_far(1, 1)
    z_near(2)
    y_send(2, 1)
    t_step(5)
    y_far(1, 3)
    y_send(2, 3)
    y_near(1, 2)
    y_far(0, 2)
    z_near(3)
    y_send(3, 1)
    y_send(3, 3)
    z_far(2)
    b_wait(0)
    y_send(2, 2)
    on(0, (0, 0))
    z_far(3)
    y_send(3, 2)
    t_step(6)
    t_last()
    on(1, (0, 0))
    y_near(2, 1)
    on(1, (1, 0))
    q_pass(0)
    q_pass(1)
    y_near(2, 3)
    y_far(1, 2)
    y_near(3, 1)
    y_near(3, 3)
    b_wait(1)
    on(0, (0, 1))
    on(1, (0, 1))
    y_near(2, 2)
    y_near(3, 2)
    on(1, (1, 1))
    y_far(2, 1)
    y_far(2, 3)
    y_far(3, 1)
    y_far(3, 3)
    y_far(2, 2)
    y_far(3, 2)
    q_last()
    on(0, (1, 0), (1, 1))
    b_wait(2)
    on(1, (0, 2), (1, 2))
    b_wait(3)
    on(0, (0, 2), (1, 2))
    unit(0, 3)
    unit(1, 3)
    peak_out(0)
    peak_out(1)
    out_move(0, G - 1)
    out_move(1, G - 1)

    s1_each(s1_sent)
    for q in range(8 - ND):
        t_send(q).wait_send()

    @pl.when(c == 1)
    def _():
        for q in range(8 - NQ):
            relay(q).wait_send()
        for slot in range(2):
            for q in range(ND):
                t_copy(slot, q).wait_send()

    @pl.when(c == 0)
    def _():
        for q in range(NQ):
            opp_copy(q).wait_send()

    for g in range(G):
        for d in range(2):
            z_copy(g, d).wait_send()
            z_relay(g, d).wait_send()
            for r in rels:
                y_copy(g, r, d).wait_send()
                y_relay(g, r, d).wait_send()
        for r in rels:
            b_copy(g, r, c).wait_send()

    for i in range(8):
        ref = precv.at[i]
        rc(ref, ref, p_ss.at[0], p_rs.at[i], sib).wait_recv()
    top = precv[0]
    for i in range(1, 8):
        top = jnp.maximum(top, precv[i])
    top = top + 1e-06
    scale_ref[...] = top[0, :TOK]
    inverse = 1.0 / top
    for p in range(2):
        for g in range(G):
            ref = orecv.at[:, pl.ds(p * PIECE + START[g], WIDTH[g])]
            rc(ref, ref, o_ss.at[0], o_rs.at[p * G + g], sib).wait_recv()
    for i in range(PAD // ROWS):
        n = min(ROWS, TOK - i * ROWS)
        inv = jnp.broadcast_to(inverse[:1, i * ROWS:(i + 1) * ROWS], (ROWS, ROWS)).T
        for k in range(NCOL // 128):
            val = orecv[pl.ds(i * ROWS, ROWS), pl.ds(k * 128, 128)].astype(jnp.float32) * inv
            out_ref[pl.ds(i * ROWS, n), pl.ds(k * 128, 128)] = val.astype(jnp.bfloat16)[:n]

    for slot in range(2):
        for g in range(G):
            out_move(slot, g, True)
        peak_move(slot, True)


def shards(tokens, norm_gain, gate_weight, up_weight):
    dma = pltpu.SemaphoreType.DMA
    vmem = pl.BlockSpec(memory_space=pltpu.VMEM)
    hbm = pl.BlockSpec(memory_space=pl.ANY)
    return pl.pallas_call(
        kernel,
        name="block",
        out_shape=(jax.ShapeDtypeStruct((TOK, NCOL), jnp.bfloat16),
                   jax.ShapeDtypeStruct((TOK,), jnp.float32)),
        in_specs=[hbm, vmem, hbm, hbm],
        out_specs=(vmem, vmem),
        scratch_shapes=[
            pltpu.VMEM((TOK, D), jnp.bfloat16),
            pltpu.VMEM((3, PAD, D), jnp.bfloat16),
            *[pltpu.VMEM((16, 2, 128, 2 * n), jnp.bfloat16) for n in WIDTH],
            pltpu.VMEM((2, PAD, 128), jnp.float32),
            pltpu.VMEM((2, PAD, PIECE), jnp.bfloat16),
            pltpu.VMEM((PAD, NCOL), jnp.bfloat16),
            pltpu.VMEM((2, 8, PAD), jnp.float32),
            pltpu.VMEM((8, 8, PAD), jnp.float32),
            dma, dma((G * 4,)), dma((G * 4,)), dma((8,)), dma((16,)), dma((4,)), dma((8,)), dma((8,)),
            dma((2,)), dma((G * 4,)), dma((G * 4,)), dma((G * 16,)), dma((G * 16,)),
            dma((G * 4,)), dma((G * 4,)), dma((2 * G,)), dma((2 * G,)), dma((8,)), dma((8,)),
        ],
        compiler_params=pltpu.CompilerParams(
            collective_id=0, has_side_effects=True, vmem_limit_bytes=58 * 2**20),
    )(tokens, norm_gain, gate_weight, up_weight)


def solution(mesh):
    in_specs = (P("seq", None), P(), P("seq", "tp"), P("seq", "tp"))
    out_specs = (P("seq", "tp"), P("seq"))
    return jax.shard_map(shards, mesh=mesh, in_specs=in_specs, out_specs=out_specs, check_vma=False)
```

```python
import jax
import jax.numpy as jnp
from jax import lax
from jax.experimental import pallas as pl
from jax.experimental.pallas import tpu as pltpu
from jax.sharding import PartitionSpec as P

MESH = pl.DeviceIdType.MESH
TOK = 504
PAD = 512
D = 4096
PIECE = 896
NCOL = 2 * PIECE
ROWS = 128
EPS = 1e-05
WIDTH = (256, 256, 256, 128)
START = (0, 256, 512, 768)
G = len(WIDTH)
ND, NQ = 1, 2


def mod(v, n):
    return lax.rem(v + 2 * n, n)


def kernel(tok_hbm, gain_ref, gate_hbm, up_hbm, orecv, top_ref,
           raw, tok, *rest):
    w = rest[:G]
    (peak, osend, psend, precv, raw_sem, s1_ss, s1_rs, t_ss, t_rs, f_ss, r_ss, r_rs, q_ss,
     z_ss, z_rs, y_ss, y_rs, b_ss, b_rs, o_ss, o_rs, p_ss, p_rs) = rest[G:]
    s = lax.axis_index("seq")
    t = lax.axis_index("tp")
    x = s % 4
    zh = (s // 4) % 4
    y = s // 16
    zl = t // 2
    c = t % 2

    def dev(xx, yy, zz, ll, cc):
        return ((yy * 4 + zz) * 4 + xx, ll * 2 + cc)

    def rc(src, dst, ssem, rsem, target):
        return pltpu.make_async_remote_copy(
            src_ref=src, dst_ref=dst, send_sem=ssem, recv_sem=rsem,
            device_id=target, device_id_type=MESH)

    xp, xm = mod(x + 1, 4), mod(x - 1, 4)
    yp, ym = mod(y + 1, 4), mod(y - 1, 4)
    zp, zm = mod(zh + 1, 4), mod(zh - 1, 4)
    sib = dev(x, y, zh, zl, 1 - c)
    pair = dev(x, y, zh, 1 - zl, c)
    y_up, y_dn = dev(x, yp, zh, zl, c), dev(x, ym, zh, zl, c)
    z_up, z_dn = dev(x, y, zp, zl, c), dev(x, y, zm, zl, c)

    raw_copy = pltpu.make_async_copy(tok_hbm, raw, raw_sem)
    raw_copy.start()

    barrier = pltpu.get_barrier_semaphore()
    for dx in range(4):
        for ll in range(2):
            for cc in range(2):
                if dx == 0 and ll == 0 and cc == 0:
                    continue
                pl.semaphore_signal(
                    barrier, inc=1, device_id_type=MESH,
                    device_id=dev(mod(x + dx, 4), y, zh, (zl + ll) % 2, (c + cc) % 2))
    for target in (y_up, y_dn, z_up, z_dn):
        pl.semaphore_signal(barrier, inc=1, device_id=target, device_id_type=MESH)

    raw_copy.wait()
    gain = gain_ref[...].reshape(1, D)

    def normed(values):
        v = values.astype(jnp.float32)
        mean_square = jnp.sum(v * v, axis=1, keepdims=True) * (1.0 / D)
        return (v * lax.rsqrt(mean_square + EPS) * gain).astype(jnp.bfloat16)

    def put(r, n, val):
        for yy in range(4):
            for zz in range(4):
                a, b = (yy * 4 + zz) * 256, (zz * 4 + yy) * 256
                tok[2, pl.ds(r, n), pl.ds(b, 256)] = val[:, a:a + 256]

    def norm_group(i, carry):
        r = pl.multiple_of(i * 16, 16)
        put(r, 16, normed(raw[pl.ds(r, 16), :]))
        return carry

    lax.fori_loop(0, 31, norm_group, 0)
    tail = normed(raw[pl.ds(496, 8), :])
    put(496, 16, jnp.concatenate([tail, jnp.zeros((8, D), jnp.bfloat16)], axis=0))
    peak[...] = jnp.zeros_like(peak)

    pl.semaphore_wait(barrier, 19)

    def chunk(g, zz, yy, cc):
        return w[g].at[zz * 4 + yy, cc]

    def half(g, zz, yy, hh):
        return w[g].at[zz * 4 + yy, c, pl.ds(hh * 64, 64)]

    def s1_dst(g, xx, u):
        return w[g].at[zh * 4 + y, xx // 2, pl.ds(pl.multiple_of((xx % 2) * 64, 64), 64),
                       pl.ds(u * WIDTH[g], WIDTH[g])]

    def s1_copy(g, h, u):
        src = (gate_hbm, up_hbm)[u].at[:, pl.ds(h * PIECE + START[g], WIDTH[g])]
        return src, s1_dst(g, x, u), s1_rs.at[g * 4 + (x % 2) * 2 + u]

    def s1_each(act):
        for g in range(G):
            for h in range(2):
                mine = jnp.logical_and(x // 2 == c, x % 2 == h)
                for u in range(2):
                    act(g, h, u, mine)

    def s1_start(g, h, u, mine):
        src, dst, sem = s1_copy(g, h, u)

        @pl.when(mine)
        def _():
            pltpu.make_async_copy(src, dst, sem).start()

        @pl.when(jnp.logical_not(mine))
        def _():
            rc(src, dst, s1_ss.at[g * 4 + h * 2 + u], sem, dev(2 * c + h, y, zh, zl, x // 2)).start()

    def s1_sent(g, h, u, mine):
        src, dst, sem = s1_copy(g, h, u)

        @pl.when(jnp.logical_not(mine))
        def _():
            rc(src, dst, s1_ss.at[g * 4 + h * 2 + u], sem, sib).wait_send()

    s1_each(s1_start)

    def tok_half(slot, q):
        return tok.at[slot, pl.ds(pl.multiple_of(jnp.where(zl == 0, q, 7 - q) * 64, 64), 64)]

    t_target = dev(mod(x + 1 - 2 * c, 4), y, zh, zl, 1)

    def t_send(q):
        return rc(tok_half(2, q), tok_half(c, q), t_ss.at[q], t_rs.at[c * 8 + q], t_target)

    def x_send(q):
        t_send(q).start()

    def t_arrived(slot, q):
        ref = tok_half(slot, q)
        rc(ref, ref, t_ss.at[0], t_rs.at[slot * 8 + q], sib).wait_recv()

    def t_copy(slot, q):
        ref = tok_half(slot, q)
        return rc(ref, ref, f_ss.at[slot * 2 + q], t_rs.at[slot * 8 + 7 - q], pair)

    def relay(q):
        slot = q % 2
        target = dev((xp, xm)[slot], y, zh, zl, 0)
        return rc(tok_half(slot, q), tok_half(1, q), r_ss.at[q], r_rs.at[q], target)

    def opp_arrived(q):
        ref = tok_half(1, q)
        rc(ref, ref, r_ss.at[0], r_rs.at[q], sib).wait_recv()

    def opp_copy(q):
        ref = tok_half(1, q)
        return rc(ref, ref, q_ss.at[q], r_rs.at[7 - q], pair)

    def t_step(q):
        @pl.when(c == 1)
        def _():
            for slot in range(2):
                t_arrived(slot, q)
            if q < 8 - NQ:
                relay(q).start()

    def t_pass(slot, q):
        @pl.when(c == 1)
        def _():
            t_copy(slot, q).start()

    def t_last():
        @pl.when(c == 1)
        def _():
            for slot in range(2):
                for q in range(8 - ND, 8):
                    t_arrived(slot, q)

    def q_pass(q):
        @pl.when(c == 0)
        def _():
            opp_arrived(q)
            opp_copy(q).start()

    def q_mid():
        @pl.when(c == 0)
        def _():
            for q in range(NQ, 4):
                opp_arrived(q)

    def q_last():
        @pl.when(c == 0)
        def _():
            for q in range(4, 8):
                opp_arrived(q)

    rels = (0, 1, 3, 2)
    zz_of = {r: mod(zh + r, 4) for r in rels}
    yy_of = {0: y, 1: yp, 3: ym, 2: mod(y + 2, 4)}

    def b_copy(g, r, cc):
        ref = w[g].at[pl.ds(pl.multiple_of(zz_of[r] * 4, 4), 4), cc]
        return rc(ref, ref, b_ss.at[g * 4 + r], b_rs.at[g * 4 + r], sib)

    def b_wait(g):
        for r in rels:
            b_copy(g, r, 1 - c).wait_recv()

    def y_copy(g, r, d):
        ref = chunk(g, zz_of[r], y, c)
        i = (g * 4 + r) * 4 + d
        return rc(ref, ref, y_ss.at[i], y_rs.at[i], (y_up, y_dn)[d])

    def y_relay(g, r, d):
        ref = half(g, zz_of[r], (ym, yp)[d], d)
        i = (g * 4 + r) * 4 + 2 + d
        return rc(ref, ref, y_ss.at[i], y_rs.at[i], (y_up, y_dn)[d])

    def z_copy(g, d):
        ref = chunk(g, zh, y, c)
        return rc(ref, ref, z_ss.at[g * 4 + d], z_rs.at[g * 4 + d], (z_up, z_dn)[d])

    def z_relay(g, d):
        ref = half(g, (zm, zp)[d], y, d)
        return rc(ref, ref, z_ss.at[g * 4 + 2 + d], z_rs.at[g * 4 + 2 + d], (z_up, z_dn)[d])

    def own(g):
        for p in range(2):
            for u in range(2):
                ref = s1_dst(g, 2 * c + p, u)
                rc(ref, ref, s1_ss.at[0], s1_rs.at[g * 4 + p * 2 + u], sib).wait_recv()

    def z_send(g):
        for d in range(2):
            z_copy(g, d).start()

    def z_near(g):
        for d in range(2):
            ref = chunk(g, (zm, zp)[d], y, c)
            rc(ref, ref, z_ss.at[0], z_rs.at[g * 4 + d], sib).wait_recv()
            z_relay(g, d).start()

    def z_far(g):
        for d in range(2):
            ref = half(g, zz_of[2], y, d)
            rc(ref, ref, z_ss.at[0], z_rs.at[g * 4 + 2 + d], sib).wait_recv()

    def y_send(g, r):
        for d in range(2):
            y_copy(g, r, d).start()

    def y_near(g, r):
        for d in range(2):
            ref = chunk(g, zz_of[r], (ym, yp)[d], c)
            rc(ref, ref, y_ss.at[0], y_rs.at[(g * 4 + r) * 4 + d], sib).wait_recv()
            y_relay(g, r, d).start()

    def y_far(g, r):
        for d in range(2):
            ref = half(g, zz_of[r], yy_of[2], d)
            rc(ref, ref, y_ss.at[0], y_rs.at[(g * 4 + r) * 4 + 2 + d], sib).wait_recv()
        b_copy(g, r, c).start()

    first = jnp.where(c == 0, 2, 0)
    rel_of = (jnp.where(c == 0, 0, 3), jnp.where(c == 0, 2, 1))

    def move(rel, src, dst, ssem, rsem, ll, cc, wait):
        here = jnp.logical_and(rel == 0, jnp.logical_and(ll == zl, cc == c))

        @pl.when(jnp.logical_not(here))
        def _():
            copy = rc(src, dst, ssem, rsem, dev(mod(x + rel, 4), y, zh, ll, cc))
            if wait:
                copy.wait_send()
            else:
                copy.start()

        if not wait:
            @pl.when(here)
            def _():
                pltpu.make_async_copy(src, dst, rsem).start()

    def out_move(slot, g, wait=False):
        n = WIDTH[g]
        dst = orecv.at[:, pl.ds(pl.multiple_of((x % 2) * PIECE + START[g], 128), n)]
        move(rel_of[slot], osend.at[slot, :, pl.ds(START[g], n)], dst,
             o_ss.at[slot * G + g], o_rs.at[(x % 2) * G + g], zl, x // 2, wait)

    def peak_move(slot, wait=False):
        index = rel_of[slot] * 2 + zl
        for k in range(4):
            move(rel_of[slot], psend.at[slot], precv.at[index],
                 p_ss.at[slot * 4 + k], p_rs.at[index], k // 2, k % 2, wait)

    def unit(slot, g, part=None):
        n = WIDTH[g]
        src = first if slot == 0 else 1
        rows = pl.ds(0, PAD) if part is None else pl.ds(
            pl.multiple_of(jnp.where(zl == 0, part, 1 - part) * 256, 256), 256)
        res = jnp.dot(tok[src, rows], w[g][...].reshape(D, 2 * n), preferred_element_type=jnp.float32)
        gate, up = res[:, :n], res[:, n:]
        val = gate / (1.0 + jnp.exp(-gate)) * up
        top = peak[slot, rows]
        for k in range(0, n, 128):
            top = jnp.maximum(top, jnp.abs(val[:, k:k + 128]))
        peak[slot, rows] = top
        osend[slot, rows, pl.ds(START[g], n)] = val.astype(jnp.bfloat16)
        if g < G - 1 and part != 0:
            out_move(slot, g)

    def on(core, *calls):
        @pl.when(c == core)
        def _():
            for call in calls:
                unit(*call)

    def peak_out(slot):
        for i in range(4):
            r = pl.ds(i * 128, 128)
            top = jnp.max(peak[slot, r].T, axis=0, keepdims=True)
            psend[slot, :, r] = jnp.broadcast_to(top, (8, 128))
        peak_move(slot)

    x_send(0)
    own(0)
    y_send(0, 0)
    z_send(0)
    x_send(1)
    own(1)
    y_send(1, 0)
    own(2)
    y_send(2, 0)
    own(3)
    y_send(3, 0)
    y_near(0, 0)
    x_send(2)
    y_near(1, 0)
    z_send(1)
    z_near(0)
    y_send(0, 3)
    t_step(0)
    y_send(0, 1)
    y_near(2, 0)
    y_near(3, 0)
    y_far(0, 0)
    t_step(1)
    z_near(1)
    y_send(1, 3)
    z_far(0)
    y_far(1, 0)
    x_send(3)
    z_send(2)
    y_near(0, 3)
    y_send(0, 2)
    t_step(2)
    y_near(0, 1)
    y_far(2, 0)
    z_far(1)
    y_send(1, 1)
    y_far(3, 0)
    z_send(3)
    z_near(2)
    y_send(1, 2)
    y_near(1, 3)
    t_pass(0, 0)
    x_send(4)
    z_near(3)
    y_far(0, 3)
    z_far(2)
    y_near(0, 2)
    t_step(3)
    y_far(0, 1)
    y_near(1, 1)
    x_send(5)
    q_pass(0)
    y_send(2, 3)
    z_far(3)
    y_near(1, 2)
    y_far(1, 3)
    y_send(2, 1)
    x_send(6)
    t_pass(1, 0)
    y_send(2, 2)
    t_step(4)
    y_far(0, 2)
    y_send(3, 3)
    b_wait(0)
    y_far(1, 1)
    on(0, (0, 0))
    y_send(3, 1)
    y_near(2, 3)
    y_send(3, 2)
    t_step(5)
    q_pass(1)
    y_far(1, 2)
    y_near(2, 1)
    b_wait(1)
    on(0, (0, 1))
    y_near(2, 2)
    t_step(6)
    t_last()
    on(1, (0, 0))
    q_mid()
    on(0, (1, 0, 0))
    y_far(2, 3)
    y_near(3, 3)
    y_near(3, 1)
    y_near(3, 2)
    on(1, (1, 0))
    on(0, (1, 1, 0))
    q_last()
    on(0, (1, 0, 1))
    y_far(2, 1)
    y_far(2, 2)
    on(0, (1, 1, 1))
    y_far(3, 3)
    y_far(3, 1)
    y_far(3, 2)
    on(1, (0, 1))
    b_wait(2)
    on(0, (0, 2))
    on(1, (1, 1))
    b_wait(3)
    on(0, (1, 2, 0), (1, 2, 1), (1, 3, 0), (1, 3, 1))
    on(1, (0, 2), (1, 2), (1, 3))
    unit(0, 3)
    peak_out(0)
    peak_out(1)
    out_move(0, G - 1)
    out_move(1, G - 1)

    s1_each(s1_sent)
    for q in range(8 - ND):
        t_send(q).wait_send()

    @pl.when(c == 1)
    def _():
        for q in range(8 - NQ):
            relay(q).wait_send()
        for slot in range(2):
            for q in range(ND):
                t_copy(slot, q).wait_send()

    @pl.when(c == 0)
    def _():
        for q in range(NQ):
            opp_copy(q).wait_send()

    for g in range(G):
        for d in range(2):
            z_copy(g, d).wait_send()
            z_relay(g, d).wait_send()
            for r in rels:
                y_copy(g, r, d).wait_send()
                y_relay(g, r, d).wait_send()
        for r in rels:
            b_copy(g, r, c).wait_send()

    for i in range(8):
        ref = precv.at[i]
        rc(ref, ref, p_ss.at[0], p_rs.at[i], sib).wait_recv()
    top = precv[0]
    for i in range(1, 8):
        top = jnp.maximum(top, precv[i])
    top_ref[...] = top + 1e-06
    for p in range(2):
        for g in range(G):
            ref = orecv.at[:, pl.ds(p * PIECE + START[g], WIDTH[g])]
            rc(ref, ref, o_ss.at[0], o_rs.at[p * G + g], sib).wait_recv()

    for slot in range(2):
        for g in range(G):
            out_move(slot, g, True)
        peak_move(slot, True)


def rescale(hidden_ref, top_ref, all_ref, out_ref, scale_ref):
    inv = jnp.broadcast_to(1.0 / top_ref[:1, :], (ROWS, ROWS)).T
    for k in range(0, NCOL, 128):
        cols = pl.ds(k, 128)
        out_ref[:, cols] = (hidden_ref[:, cols].astype(jnp.float32) * inv).astype(jnp.bfloat16)

    @pl.when(pl.program_id(0) == 0)
    def _():
        scale_ref[...] = all_ref[0, :TOK]


def shards(tokens, norm_gain, gate_weight, up_weight):
    dma = pltpu.SemaphoreType.DMA
    vmem = pl.BlockSpec(memory_space=pltpu.VMEM)
    hbm = pl.BlockSpec(memory_space=pl.ANY)
    hidden, tops = pl.pallas_call(
        kernel,
        name="block",
        out_shape=(jax.ShapeDtypeStruct((PAD, NCOL), jnp.bfloat16),
                   jax.ShapeDtypeStruct((8, PAD), jnp.float32)),
        in_specs=[hbm, vmem, hbm, hbm],
        out_specs=(hbm, vmem),
        scratch_shapes=[
            pltpu.VMEM((TOK, D), jnp.bfloat16),
            pltpu.VMEM((3, PAD, D), jnp.bfloat16),
            *[pltpu.VMEM((16, 2, 128, 2 * n), jnp.bfloat16) for n in WIDTH],
            pltpu.VMEM((2, PAD, 128), jnp.float32),
            pltpu.VMEM((2, PAD, PIECE), jnp.bfloat16),
            pltpu.VMEM((2, 8, PAD), jnp.float32),
            pltpu.VMEM((8, 8, PAD), jnp.float32),
            dma, dma((G * 4,)), dma((G * 4,)), dma((8,)), dma((16,)), dma((4,)), dma((8,)), dma((8,)),
            dma((4,)), dma((G * 4,)), dma((G * 4,)), dma((G * 16,)), dma((G * 16,)),
            dma((G * 4,)), dma((G * 4,)), dma((2 * G,)), dma((2 * G,)), dma((8,)), dma((8,)),
        ],
        compiler_params=pltpu.CompilerParams(
            collective_id=0, has_side_effects=True, vmem_limit_bytes=58 * 2**20),
    )(tokens, norm_gain, gate_weight, up_weight)
    return pl.pallas_call(
        rescale,
        name="rescale",
        grid=(PAD // ROWS,),
        out_shape=(jax.ShapeDtypeStruct((TOK, NCOL), jnp.bfloat16),
                   jax.ShapeDtypeStruct((TOK,), jnp.float32)),
        in_specs=[pl.BlockSpec((ROWS, NCOL), lambda i: (i, 0)),
                  pl.BlockSpec((8, ROWS), lambda i: (0, i)),
                  pl.BlockSpec((8, PAD), lambda i: (0, 0))],
        out_specs=(pl.BlockSpec((ROWS, NCOL), lambda i: (i, 0)),
                   pl.BlockSpec((TOK,), lambda i: (0,))),
    )(hidden, tops, tops)


def solution(mesh):
    in_specs = (P("seq", None), P(), P("seq", "tp"), P("seq", "tp"))
    out_specs = (P("seq", "tp"), P("seq"))
    return jax.shard_map(shards, mesh=mesh, in_specs=in_specs, out_specs=out_specs, check_vma=False)
```

```python
import jax
import jax.numpy as jnp
from jax import lax
from jax.experimental import pallas as pl
from jax.experimental.pallas import tpu as pltpu
from jax.sharding import PartitionSpec as P

MESH = pl.DeviceIdType.MESH
TOK = 504
PAD = 512
D = 4096
PIECE = 896
NCOL = 2 * PIECE
ROWS = 128
BLOCK = 256
EPS = 1e-05
WIDTH = (256, 256, 256, 128)
START = (0, 256, 512, 768)
G = len(WIDTH)
ND, NQ = 1, 2


def mod(v, n):
    return lax.rem(v + 2 * n, n)


def kernel(tok_hbm, gain_ref, gate_hbm, up_hbm, orecv, top_ref,
           raw, tok, *rest):
    w = rest[:G]
    (peak, osend, psend, precv, raw_sem, s1_ss, s1_rs, t_ss, t_rs, f_ss, r_ss, r_rs, q_ss,
     z_ss, z_rs, y_ss, y_rs, b_ss, b_rs, o_ss, o_rs, p_ss, p_rs) = rest[G:]
    s = lax.axis_index("seq")
    t = lax.axis_index("tp")
    x = s % 4
    zh = (s // 4) % 4
    y = s // 16
    zl = t // 2
    c = t % 2

    def dev(xx, yy, zz, ll, cc):
        return ((yy * 4 + zz) * 4 + xx, ll * 2 + cc)

    def rc(src, dst, ssem, rsem, target):
        return pltpu.make_async_remote_copy(
            src_ref=src, dst_ref=dst, send_sem=ssem, recv_sem=rsem,
            device_id=target, device_id_type=MESH)

    xp, xm = mod(x + 1, 4), mod(x - 1, 4)
    yp, ym = mod(y + 1, 4), mod(y - 1, 4)
    zp, zm = mod(zh + 1, 4), mod(zh - 1, 4)
    sib = dev(x, y, zh, zl, 1 - c)
    pair = dev(x, y, zh, 1 - zl, c)
    y_up, y_dn = dev(x, yp, zh, zl, c), dev(x, ym, zh, zl, c)
    z_up, z_dn = dev(x, y, zp, zl, c), dev(x, y, zm, zl, c)

    raw_copy = pltpu.make_async_copy(tok_hbm, raw, raw_sem)
    raw_copy.start()

    barrier = pltpu.get_barrier_semaphore()
    for dx in range(4):
        for ll in range(2):
            for cc in range(2):
                if dx == 0 and ll == 0 and cc == 0:
                    continue
                pl.semaphore_signal(
                    barrier, inc=1, device_id_type=MESH,
                    device_id=dev(mod(x + dx, 4), y, zh, (zl + ll) % 2, (c + cc) % 2))
    for target in (y_up, y_dn, z_up, z_dn):
        pl.semaphore_signal(barrier, inc=1, device_id=target, device_id_type=MESH)

    raw_copy.wait()
    gain = gain_ref[...].reshape(1, D)

    def normed(values):
        v = values.astype(jnp.float32)
        mean_square = jnp.sum(v * v, axis=1, keepdims=True) * (1.0 / D)
        return (v * lax.rsqrt(mean_square + EPS) * gain).astype(jnp.bfloat16)

    def put(r, n, val):
        for yy in range(4):
            for zz in range(4):
                a, b = (yy * 4 + zz) * 256, (zz * 4 + yy) * 256
                tok[2, pl.ds(r, n), pl.ds(b, 256)] = val[:, a:a + 256]

    def norm_group(i, carry):
        r = pl.multiple_of(i * 16, 16)
        put(r, 16, normed(raw[pl.ds(r, 16), :]))
        return carry

    lax.fori_loop(0, 31, norm_group, 0)
    tail = normed(raw[pl.ds(496, 8), :])
    put(496, 16, jnp.concatenate([tail, jnp.zeros((8, D), jnp.bfloat16)], axis=0))
    peak[...] = jnp.zeros_like(peak)

    pl.semaphore_wait(barrier, 19)

    def chunk(g, zz, yy, cc):
        return w[g].at[zz * 4 + yy, cc]

    def half(g, zz, yy, hh):
        return w[g].at[zz * 4 + yy, c, pl.ds(hh * 64, 64)]

    def s1_dst(g, xx, u):
        return w[g].at[zh * 4 + y, xx // 2, pl.ds(pl.multiple_of((xx % 2) * 64, 64), 64),
                       pl.ds(u * WIDTH[g], WIDTH[g])]

    def s1_copy(g, h, u):
        src = (gate_hbm, up_hbm)[u].at[:, pl.ds(h * PIECE + START[g], WIDTH[g])]
        return src, s1_dst(g, x, u), s1_rs.at[g * 4 + (x % 2) * 2 + u]

    def s1_each(act):
        for g in range(G):
            for h in range(2):
                mine = jnp.logical_and(x // 2 == c, x % 2 == h)
                for u in range(2):
                    act(g, h, u, mine)

    def s1_start(g, h, u, mine):
        src, dst, sem = s1_copy(g, h, u)

        @pl.when(mine)
        def _():
            pltpu.make_async_copy(src, dst, sem).start()

        @pl.when(jnp.logical_not(mine))
        def _():
            rc(src, dst, s1_ss.at[g * 4 + h * 2 + u], sem, dev(2 * c + h, y, zh, zl, x // 2)).start()

    def s1_sent(g, h, u, mine):
        src, dst, sem = s1_copy(g, h, u)

        @pl.when(jnp.logical_not(mine))
        def _():
            rc(src, dst, s1_ss.at[g * 4 + h * 2 + u], sem, sib).wait_send()

    s1_each(s1_start)

    def tok_half(slot, q):
        return tok.at[slot, pl.ds(pl.multiple_of(jnp.where(zl == 0, q, 7 - q) * 64, 64), 64)]

    t_target = dev(mod(x + 1 - 2 * c, 4), y, zh, zl, 1)

    def t_send(q):
        return rc(tok_half(2, q), tok_half(c, q), t_ss.at[q], t_rs.at[c * 8 + q], t_target)

    def x_send(q):
        t_send(q).start()

    def t_arrived(slot, q):
        ref = tok_half(slot, q)
        rc(ref, ref, t_ss.at[0], t_rs.at[slot * 8 + q], sib).wait_recv()

    def t_copy(slot, q):
        ref = tok_half(slot, q)
        return rc(ref, ref, f_ss.at[slot * 2 + q], t_rs.at[slot * 8 + 7 - q], pair)

    def relay(q):
        slot = q % 2
        target = dev((xp, xm)[slot], y, zh, zl, 0)
        return rc(tok_half(slot, q), tok_half(1, q), r_ss.at[q], r_rs.at[q], target)

    def opp_arrived(q):
        ref = tok_half(1, q)
        rc(ref, ref, r_ss.at[0], r_rs.at[q], sib).wait_recv()

    def opp_copy(q):
        ref = tok_half(1, q)
        return rc(ref, ref, q_ss.at[q], r_rs.at[7 - q], pair)

    def t_step(q):
        @pl.when(c == 1)
        def _():
            for slot in range(2):
                t_arrived(slot, q)
            if q < 8 - NQ:
                relay(q).start()

    def t_pass(slot, q):
        @pl.when(c == 1)
        def _():
            t_copy(slot, q).start()

    def t_last():
        @pl.when(c == 1)
        def _():
            for slot in range(2):
                for q in range(8 - ND, 8):
                    t_arrived(slot, q)

    def q_pass(q):
        @pl.when(c == 0)
        def _():
            opp_arrived(q)
            opp_copy(q).start()

    def q_mid():
        @pl.when(c == 0)
        def _():
            for q in range(NQ, 4):
                opp_arrived(q)

    def q_last():
        @pl.when(c == 0)
        def _():
            for q in range(4, 8):
                opp_arrived(q)

    rels = (0, 1, 3, 2)
    zz_of = {r: mod(zh + r, 4) for r in rels}
    yy_of = {0: y, 1: yp, 3: ym, 2: mod(y + 2, 4)}

    def b_copy(g, r, cc):
        ref = w[g].at[pl.ds(pl.multiple_of(zz_of[r] * 4, 4), 4), cc]
        return rc(ref, ref, b_ss.at[g * 4 + r], b_rs.at[g * 4 + r], sib)

    def b_wait(g):
        for r in rels:
            b_copy(g, r, 1 - c).wait_recv()

    def y_copy(g, r, d):
        ref = chunk(g, zz_of[r], y, c)
        i = (g * 4 + r) * 4 + d
        return rc(ref, ref, y_ss.at[i], y_rs.at[i], (y_up, y_dn)[d])

    def y_relay(g, r, d):
        ref = half(g, zz_of[r], (ym, yp)[d], d)
        i = (g * 4 + r) * 4 + 2 + d
        return rc(ref, ref, y_ss.at[i], y_rs.at[i], (y_up, y_dn)[d])

    def z_copy(g, d):
        ref = chunk(g, zh, y, c)
        return rc(ref, ref, z_ss.at[g * 4 + d], z_rs.at[g * 4 + d], (z_up, z_dn)[d])

    def z_relay(g, d):
        ref = half(g, (zm, zp)[d], y, d)
        return rc(ref, ref, z_ss.at[g * 4 + 2 + d], z_rs.at[g * 4 + 2 + d], (z_up, z_dn)[d])

    def own(g):
        for p in range(2):
            for u in range(2):
                ref = s1_dst(g, 2 * c + p, u)
                rc(ref, ref, s1_ss.at[0], s1_rs.at[g * 4 + p * 2 + u], sib).wait_recv()

    def z_send(g):
        for d in range(2):
            z_copy(g, d).start()

    def z_near(g):
        for d in range(2):
            ref = chunk(g, (zm, zp)[d], y, c)
            rc(ref, ref, z_ss.at[0], z_rs.at[g * 4 + d], sib).wait_recv()
            z_relay(g, d).start()

    def z_far(g):
        for d in range(2):
            ref = half(g, zz_of[2], y, d)
            rc(ref, ref, z_ss.at[0], z_rs.at[g * 4 + 2 + d], sib).wait_recv()

    def y_send(g, r):
        for d in range(2):
            y_copy(g, r, d).start()

    def y_near(g, r):
        for d in range(2):
            ref = chunk(g, zz_of[r], (ym, yp)[d], c)
            rc(ref, ref, y_ss.at[0], y_rs.at[(g * 4 + r) * 4 + d], sib).wait_recv()
            y_relay(g, r, d).start()

    def y_far(g, r):
        for d in range(2):
            ref = half(g, zz_of[r], yy_of[2], d)
            rc(ref, ref, y_ss.at[0], y_rs.at[(g * 4 + r) * 4 + 2 + d], sib).wait_recv()
        b_copy(g, r, c).start()

    first = jnp.where(c == 0, 2, 0)
    rel_of = (jnp.where(c == 0, 0, 3), jnp.where(c == 0, 2, 1))

    def move(rel, src, dst, ssem, rsem, ll, cc, wait):
        here = jnp.logical_and(rel == 0, jnp.logical_and(ll == zl, cc == c))

        @pl.when(jnp.logical_not(here))
        def _():
            copy = rc(src, dst, ssem, rsem, dev(mod(x + rel, 4), y, zh, ll, cc))
            if wait:
                copy.wait_send()
            else:
                copy.start()

        if not wait:
            @pl.when(here)
            def _():
                pltpu.make_async_copy(src, dst, rsem).start()

    def out_move(slot, g, wait=False):
        n = WIDTH[g]
        dst = orecv.at[:, pl.ds(pl.multiple_of((x % 2) * PIECE + START[g], 128), n)]
        move(rel_of[slot], osend.at[slot, :, pl.ds(START[g], n)], dst,
             o_ss.at[slot * G + g], o_rs.at[(x % 2) * G + g], zl, x // 2, wait)

    def peak_move(slot, wait=False):
        index = rel_of[slot] * 2 + zl
        for k in range(4):
            move(rel_of[slot], psend.at[slot], precv.at[index],
                 p_ss.at[slot * 4 + k], p_rs.at[index], k // 2, k % 2, wait)

    def unit(slot, g, part=None):
        n = WIDTH[g]
        src = first if slot == 0 else 1
        rows = pl.ds(0, PAD) if part is None else pl.ds(
            pl.multiple_of(jnp.where(zl == 0, part, 1 - part) * 256, 256), 256)
        res = jnp.dot(tok[src, rows], w[g][...].reshape(D, 2 * n), preferred_element_type=jnp.float32)
        gate, up = res[:, :n], res[:, n:]
        val = gate / (1.0 + jnp.exp(-gate)) * up
        top = peak[slot, rows]
        for k in range(0, n, 128):
            top = jnp.maximum(top, jnp.abs(val[:, k:k + 128]))
        peak[slot, rows] = top
        osend[slot, rows, pl.ds(START[g], n)] = val.astype(jnp.bfloat16)
        if part != 0:
            out_move(slot, g)

    def on(core, *calls):
        @pl.when(c == core)
        def _():
            for call in calls:
                unit(*call)

    def peak_out(slot):
        for i in range(4):
            r = pl.ds(i * 128, 128)
            top = jnp.max(peak[slot, r].T, axis=0, keepdims=True)
            psend[slot, :, r] = jnp.broadcast_to(top, (8, 128))
        peak_move(slot)

    x_send(0)
    own(0)
    y_send(0, 0)
    z_send(0)
    x_send(1)
    own(1)
    y_send(1, 0)
    own(2)
    y_send(2, 0)
    own(3)
    y_send(3, 0)
    y_near(0, 0)
    x_send(2)
    z_send(1)
    y_near(1, 0)
    z_near(0)
    y_send(0, 3)
    t_step(0)
    y_send(0, 1)
    y_near(2, 0)
    y_near(3, 0)
    y_far(0, 0)
    t_step(1)
    z_near(1)
    y_send(1, 3)
    z_far(0)
    y_far(1, 0)
    x_send(3)
    z_send(2)
    y_near(0, 3)
    y_send(0, 2)
    t_step(2)
    y_near(0, 1)
    y_far(2, 0)
    z_far(1)
    y_send(1, 1)
    y_far(3, 0)
    z_send(3)
    z_near(2)
    y_send(1, 2)
    y_near(1, 3)
    t_pass(0, 0)
    x_send(4)
    z_near(3)
    y_far(0, 3)
    z_far(2)
    y_near(0, 2)
    t_step(3)
    y_far(0, 1)
    y_near(1, 1)
    x_send(5)
    q_pass(0)
    y_send(2, 3)
    z_far(3)
    y_near(1, 2)
    y_far(1, 3)
    y_send(2, 1)
    x_send(6)
    t_pass(1, 0)
    y_send(2, 2)
    t_step(4)
    y_far(0, 2)
    y_send(3, 3)
    b_wait(0)
    y_far(1, 1)
    on(0, (0, 0))
    y_send(3, 1)
    y_near(2, 3)
    y_send(3, 2)
    t_step(5)
    q_pass(1)
    y_far(1, 2)
    y_near(2, 1)
    b_wait(1)
    on(0, (0, 1))
    y_near(2, 2)
    t_step(6)
    t_last()
    on(1, (0, 0))
    q_mid()
    on(0, (1, 0, 0))
    y_far(2, 3)
    y_near(3, 3)
    y_near(3, 1)
    y_near(3, 2)
    on(1, (1, 0))
    on(0, (1, 1, 0))
    q_last()
    on(0, (1, 0, 1))
    y_far(2, 1)
    y_far(2, 2)
    on(0, (1, 1, 1))
    y_far(3, 3)
    y_far(3, 1)
    y_far(3, 2)
    on(1, (0, 1))
    b_wait(2)
    on(0, (0, 2))
    on(1, (1, 1))
    b_wait(3)
    on(0, (1, 2, 0), (1, 2, 1), (1, 3, 0), (1, 3, 1))
    on(1, (0, 2), (1, 2), (1, 3))
    unit(0, 3)
    peak_out(0)
    peak_out(1)

    s1_each(s1_sent)
    for q in range(8 - ND):
        t_send(q).wait_send()

    @pl.when(c == 1)
    def _():
        for q in range(8 - NQ):
            relay(q).wait_send()
        for slot in range(2):
            for q in range(ND):
                t_copy(slot, q).wait_send()

    @pl.when(c == 0)
    def _():
        for q in range(NQ):
            opp_copy(q).wait_send()

    for g in range(G):
        for d in range(2):
            z_copy(g, d).wait_send()
            z_relay(g, d).wait_send()
            for r in rels:
                y_copy(g, r, d).wait_send()
                y_relay(g, r, d).wait_send()
        for r in rels:
            b_copy(g, r, c).wait_send()

    for i in range(8):
        ref = precv.at[i]
        rc(ref, ref, p_ss.at[0], p_rs.at[i], sib).wait_recv()
    top = precv[0]
    for i in range(1, 8):
        top = jnp.maximum(top, precv[i])
    top_ref[...] = top + 1e-06
    for p in range(2):
        for g in range(G):
            ref = orecv.at[:, pl.ds(p * PIECE + START[g], WIDTH[g])]
            rc(ref, ref, o_ss.at[0], o_rs.at[p * G + g], sib).wait_recv()

    for slot in range(2):
        for g in range(G):
            out_move(slot, g, True)
        peak_move(slot, True)


def rescale(hidden_ref, top_ref, all_ref, out_ref, scale_ref):
    for r in range(0, BLOCK, ROWS):
        rows = pl.ds(r, ROWS)
        inv = jnp.broadcast_to(1.0 / top_ref[:1, r:r + ROWS], (ROWS, ROWS)).T
        for k in range(0, NCOL, 128):
            cols = pl.ds(k, 128)
            out_ref[rows, cols] = (hidden_ref[rows, cols].astype(jnp.float32) * inv).astype(jnp.bfloat16)

    @pl.when(pl.program_id(0) == 0)
    def _():
        scale_ref[...] = all_ref[0, :TOK]


def shards(tokens, norm_gain, gate_weight, up_weight):
    dma = pltpu.SemaphoreType.DMA
    vmem = pl.BlockSpec(memory_space=pltpu.VMEM)
    hbm = pl.BlockSpec(memory_space=pl.ANY)
    hidden, tops = pl.pallas_call(
        kernel,
        name="block",
        out_shape=(jax.ShapeDtypeStruct((PAD, NCOL), jnp.bfloat16),
                   jax.ShapeDtypeStruct((8, PAD), jnp.float32)),
        in_specs=[hbm, vmem, hbm, hbm],
        out_specs=(hbm, vmem),
        scratch_shapes=[
            pltpu.VMEM((TOK, D), jnp.bfloat16),
            pltpu.VMEM((3, PAD, D), jnp.bfloat16),
            *[pltpu.VMEM((16, 2, 128, 2 * n), jnp.bfloat16) for n in WIDTH],
            pltpu.VMEM((2, PAD, 128), jnp.float32),
            pltpu.VMEM((2, PAD, PIECE), jnp.bfloat16),
            pltpu.VMEM((2, 8, PAD), jnp.float32),
            pltpu.VMEM((8, 8, PAD), jnp.float32),
            dma, dma((G * 4,)), dma((G * 4,)), dma((8,)), dma((16,)), dma((4,)), dma((8,)), dma((8,)),
            dma((4,)), dma((G * 4,)), dma((G * 4,)), dma((G * 16,)), dma((G * 16,)),
            dma((G * 4,)), dma((G * 4,)), dma((2 * G,)), dma((2 * G,)), dma((8,)), dma((8,)),
        ],
        compiler_params=pltpu.CompilerParams(
            collective_id=0, has_side_effects=True, vmem_limit_bytes=58 * 2**20),
    )(tokens, norm_gain, gate_weight, up_weight)
    return pl.pallas_call(
        rescale,
        name="rescale",
        grid=(PAD // BLOCK,),
        out_shape=(jax.ShapeDtypeStruct((TOK, NCOL), jnp.bfloat16),
                   jax.ShapeDtypeStruct((TOK,), jnp.float32)),
        in_specs=[pl.BlockSpec((BLOCK, NCOL), lambda i: (i, 0)),
                  pl.BlockSpec((8, BLOCK), lambda i: (0, i)),
                  pl.BlockSpec((8, PAD), lambda i: (0, 0))],
        out_specs=(pl.BlockSpec((BLOCK, NCOL), lambda i: (i, 0)),
                   pl.BlockSpec((TOK,), lambda i: (0,))),
    )(hidden, tops, tops)


def solution(mesh):
    in_specs = (P("seq", None), P(), P("seq", "tp"), P("seq", "tp"))
    out_specs = (P("seq", "tp"), P("seq"))
    return jax.shard_map(shards, mesh=mesh, in_specs=in_specs, out_specs=out_specs, check_vma=False)
```

```python
import jax
import jax.numpy as jnp
from jax import lax
from jax.experimental import pallas as pl
from jax.experimental.pallas import tpu as pltpu
from jax.sharding import PartitionSpec as P

MESH = pl.DeviceIdType.MESH
TOK = 504
PAD = 512
D = 4096
PIECE = 896
NCOL = 2 * PIECE
ROWS = 128
BLOCK = 256
EPS = 1e-05
WIDTH = (256, 256, 256, 128)
START = (0, 256, 512, 768)
G = len(WIDTH)
ND, NQ = 1, 2


def mod(v, n):
    return lax.rem(v + 2 * n, n)


def kernel(tok_hbm, gain_ref, gate_hbm, up_hbm, orecv, top_ref,
           raw, tok, *rest):
    w = rest[:G]
    (peak, osend, psend, precv, raw_sem, s1_ss, s1_rs, t_ss, t_rs, f_ss, r_ss, r_rs, q_ss,
     z_ss, z_rs, y_ss, y_rs, b_ss, b_rs, o_ss, o_rs, p_ss, p_rs) = rest[G:]
    s = lax.axis_index("seq")
    t = lax.axis_index("tp")
    x = s % 4
    zh = (s // 4) % 4
    y = s // 16
    zl = t // 2
    c = t % 2

    def dev(xx, yy, zz, ll, cc):
        return ((yy * 4 + zz) * 4 + xx, ll * 2 + cc)

    def rc(src, dst, ssem, rsem, target):
        return pltpu.make_async_remote_copy(
            src_ref=src, dst_ref=dst, send_sem=ssem, recv_sem=rsem,
            device_id=target, device_id_type=MESH)

    xp, xm = mod(x + 1, 4), mod(x - 1, 4)
    yp, ym = mod(y + 1, 4), mod(y - 1, 4)
    zp, zm = mod(zh + 1, 4), mod(zh - 1, 4)
    sib = dev(x, y, zh, zl, 1 - c)
    pair = dev(x, y, zh, 1 - zl, c)
    y_up, y_dn = dev(x, yp, zh, zl, c), dev(x, ym, zh, zl, c)
    z_up, z_dn = dev(x, y, zp, zl, c), dev(x, y, zm, zl, c)

    raw_copy = pltpu.make_async_copy(tok_hbm, raw, raw_sem)
    raw_copy.start()

    barrier = pltpu.get_barrier_semaphore()
    for dx in range(4):
        for ll in range(2):
            for cc in range(2):
                if dx == 0 and ll == 0 and cc == 0:
                    continue
                pl.semaphore_signal(
                    barrier, inc=1, device_id_type=MESH,
                    device_id=dev(mod(x + dx, 4), y, zh, (zl + ll) % 2, (c + cc) % 2))
    for target in (y_up, y_dn, z_up, z_dn):
        pl.semaphore_signal(barrier, inc=1, device_id=target, device_id_type=MESH)

    pl.semaphore_wait(barrier, 19)

    def chunk(g, zz, yy, cc):
        return w[g].at[zz * 4 + yy, cc]

    def half(g, zz, yy, hh):
        return w[g].at[zz * 4 + yy, c, pl.ds(hh * 64, 64)]

    def s1_dst(g, xx, u):
        return w[g].at[zh * 4 + y, xx // 2, pl.ds(pl.multiple_of((xx % 2) * 64, 64), 64),
                       pl.ds(u * WIDTH[g], WIDTH[g])]

    def s1_copy(g, h, u):
        src = (gate_hbm, up_hbm)[u].at[:, pl.ds(h * PIECE + START[g], WIDTH[g])]
        return src, s1_dst(g, x, u), s1_rs.at[g * 4 + (x % 2) * 2 + u]

    def s1_each(act):
        for g in range(G):
            for h in range(2):
                mine = jnp.logical_and(x // 2 == c, x % 2 == h)
                for u in range(2):
                    act(g, h, u, mine)

    def s1_start(g, h, u, mine):
        src, dst, sem = s1_copy(g, h, u)

        @pl.when(mine)
        def _():
            pltpu.make_async_copy(src, dst, sem).start()

        @pl.when(jnp.logical_not(mine))
        def _():
            rc(src, dst, s1_ss.at[g * 4 + h * 2 + u], sem, dev(2 * c + h, y, zh, zl, x // 2)).start()

    def s1_sent(g, h, u, mine):
        src, dst, sem = s1_copy(g, h, u)

        @pl.when(jnp.logical_not(mine))
        def _():
            rc(src, dst, s1_ss.at[g * 4 + h * 2 + u], sem, sib).wait_send()

    s1_each(s1_start)

    raw_copy.wait()
    gain = gain_ref[...].reshape(1, D)

    def normed(values):
        v = values.astype(jnp.float32)
        mean_square = jnp.sum(v * v, axis=1, keepdims=True) * (1.0 / D)
        return (v * lax.rsqrt(mean_square + EPS) * gain).astype(jnp.bfloat16)

    def put(r, n, val):
        for yy in range(4):
            for zz in range(4):
                a, b = (yy * 4 + zz) * 256, (zz * 4 + yy) * 256
                tok[2, pl.ds(r, n), pl.ds(b, 256)] = val[:, a:a + 256]

    def norm_group(i, carry):
        r = pl.multiple_of(i * 16, 16)
        put(r, 16, normed(raw[pl.ds(r, 16), :]))
        return carry

    lax.fori_loop(0, 31, norm_group, 0)
    tail = normed(raw[pl.ds(496, 8), :])
    put(496, 16, jnp.concatenate([tail, jnp.zeros((8, D), jnp.bfloat16)], axis=0))
    peak[...] = jnp.zeros_like(peak)


    def tok_half(slot, q):
        return tok.at[slot, pl.ds(pl.multiple_of(jnp.where(zl == 0, q, 7 - q) * 64, 64), 64)]

    t_target = dev(mod(x + 1 - 2 * c, 4), y, zh, zl, 1)

    def t_send(q):
        return rc(tok_half(2, q), tok_half(c, q), t_ss.at[q], t_rs.at[c * 8 + q], t_target)

    def x_send(q):
        t_send(q).start()

    def t_arrived(slot, q):
        ref = tok_half(slot, q)
        rc(ref, ref, t_ss.at[0], t_rs.at[slot * 8 + q], sib).wait_recv()

    def t_copy(slot, q):
        ref = tok_half(slot, q)
        return rc(ref, ref, f_ss.at[slot * 2 + q], t_rs.at[slot * 8 + 7 - q], pair)

    def relay(q):
        slot = q % 2
        target = dev((xp, xm)[slot], y, zh, zl, 0)
        return rc(tok_half(slot, q), tok_half(1, q), r_ss.at[q], r_rs.at[q], target)

    def opp_arrived(q):
        ref = tok_half(1, q)
        rc(ref, ref, r_ss.at[0], r_rs.at[q], sib).wait_recv()

    def opp_copy(q):
        ref = tok_half(1, q)
        return rc(ref, ref, q_ss.at[q], r_rs.at[7 - q], pair)

    def t_step(q):
        @pl.when(c == 1)
        def _():
            for slot in range(2):
                t_arrived(slot, q)
            if q < 8 - NQ:
                relay(q).start()

    def t_pass(slot, q):
        @pl.when(c == 1)
        def _():
            t_copy(slot, q).start()

    def t_last():
        @pl.when(c == 1)
        def _():
            for slot in range(2):
                for q in range(8 - ND, 8):
                    t_arrived(slot, q)

    def q_pass(q):
        @pl.when(c == 0)
        def _():
            opp_arrived(q)
            opp_copy(q).start()

    def q_mid():
        @pl.when(c == 0)
        def _():
            for q in range(NQ, 4):
                opp_arrived(q)

    def q_last():
        @pl.when(c == 0)
        def _():
            for q in range(4, 8):
                opp_arrived(q)

    rels = (0, 1, 3, 2)
    zz_of = {r: mod(zh + r, 4) for r in rels}
    yy_of = {0: y, 1: yp, 3: ym, 2: mod(y + 2, 4)}

    def b_copy(g, r, cc):
        ref = w[g].at[pl.ds(pl.multiple_of(zz_of[r] * 4, 4), 4), cc]
        return rc(ref, ref, b_ss.at[g * 4 + r], b_rs.at[g * 4 + r], sib)

    def b_wait(g):
        for r in rels:
            b_copy(g, r, 1 - c).wait_recv()

    def y_copy(g, r, d):
        ref = chunk(g, zz_of[r], y, c)
        i = (g * 4 + r) * 4 + d
        return rc(ref, ref, y_ss.at[i], y_rs.at[i], (y_up, y_dn)[d])

    def y_relay(g, r, d):
        ref = half(g, zz_of[r], (ym, yp)[d], d)
        i = (g * 4 + r) * 4 + 2 + d
        return rc(ref, ref, y_ss.at[i], y_rs.at[i], (y_up, y_dn)[d])

    def z_copy(g, d):
        ref = chunk(g, zh, y, c)
        return rc(ref, ref, z_ss.at[g * 4 + d], z_rs.at[g * 4 + d], (z_up, z_dn)[d])

    def z_relay(g, d):
        ref = half(g, (zm, zp)[d], y, d)
        return rc(ref, ref, z_ss.at[g * 4 + 2 + d], z_rs.at[g * 4 + 2 + d], (z_up, z_dn)[d])

    def own(g):
        for p in range(2):
            for u in range(2):
                ref = s1_dst(g, 2 * c + p, u)
                rc(ref, ref, s1_ss.at[0], s1_rs.at[g * 4 + p * 2 + u], sib).wait_recv()

    def z_send(g):
        for d in range(2):
            z_copy(g, d).start()

    def z_near(g):
        for d in range(2):
            ref = chunk(g, (zm, zp)[d], y, c)
            rc(ref, ref, z_ss.at[0], z_rs.at[g * 4 + d], sib).wait_recv()
            z_relay(g, d).start()

    def z_far(g):
        for d in range(2):
            ref = half(g, zz_of[2], y, d)
            rc(ref, ref, z_ss.at[0], z_rs.at[g * 4 + 2 + d], sib).wait_recv()

    def y_send(g, r):
        for d in range(2):
            y_copy(g, r, d).start()

    def y_near(g, r):
        for d in range(2):
            ref = chunk(g, zz_of[r], (ym, yp)[d], c)
            rc(ref, ref, y_ss.at[0], y_rs.at[(g * 4 + r) * 4 + d], sib).wait_recv()
            y_relay(g, r, d).start()

    def y_far(g, r):
        for d in range(2):
            ref = half(g, zz_of[r], yy_of[2], d)
            rc(ref, ref, y_ss.at[0], y_rs.at[(g * 4 + r) * 4 + 2 + d], sib).wait_recv()
        b_copy(g, r, c).start()

    first = jnp.where(c == 0, 2, 0)
    rel_of = (jnp.where(c == 0, 0, 3), jnp.where(c == 0, 2, 1))

    def move(rel, src, dst, ssem, rsem, ll, cc, wait):
        here = jnp.logical_and(rel == 0, jnp.logical_and(ll == zl, cc == c))

        @pl.when(jnp.logical_not(here))
        def _():
            copy = rc(src, dst, ssem, rsem, dev(mod(x + rel, 4), y, zh, ll, cc))
            if wait:
                copy.wait_send()
            else:
                copy.start()

        if not wait:
            @pl.when(here)
            def _():
                pltpu.make_async_copy(src, dst, rsem).start()

    def out_move(slot, g, wait=False):
        n = WIDTH[g]
        dst = orecv.at[:, pl.ds(pl.multiple_of((x % 2) * PIECE + START[g], 128), n)]
        move(rel_of[slot], osend.at[slot, :, pl.ds(START[g], n)], dst,
             o_ss.at[slot * G + g], o_rs.at[(x % 2) * G + g], zl, x // 2, wait)

    def peak_move(slot, wait=False):
        index = rel_of[slot] * 2 + zl
        for k in range(4):
            move(rel_of[slot], psend.at[slot], precv.at[index],
                 p_ss.at[slot * 4 + k], p_rs.at[index], k // 2, k % 2, wait)

    def unit(slot, g, part=None):
        n = WIDTH[g]
        src = first if slot == 0 else 1
        rows = pl.ds(0, PAD) if part is None else pl.ds(
            pl.multiple_of(jnp.where(zl == 0, part, 1 - part) * 256, 256), 256)
        res = jnp.dot(tok[src, rows], w[g][...].reshape(D, 2 * n), preferred_element_type=jnp.float32)
        gate, up = res[:, :n], res[:, n:]
        val = gate / (1.0 + jnp.exp(-gate)) * up
        top = peak[slot, rows]
        for k in range(0, n, 128):
            top = jnp.maximum(top, jnp.abs(val[:, k:k + 128]))
        peak[slot, rows] = top
        osend[slot, rows, pl.ds(START[g], n)] = val.astype(jnp.bfloat16)
        if part != 0:
            out_move(slot, g)

    def on(core, *calls):
        @pl.when(c == core)
        def _():
            for call in calls:
                unit(*call)

    def peak_out(slot):
        for i in range(4):
            r = pl.ds(i * 128, 128)
            top = jnp.max(peak[slot, r].T, axis=0, keepdims=True)
            psend[slot, :, r] = jnp.broadcast_to(top, (8, 128))
        peak_move(slot)

    x_send(0)
    own(0)
    y_send(0, 0)
    z_send(0)
    x_send(1)
    own(1)
    y_send(1, 0)
    own(2)
    y_send(2, 0)
    own(3)
    y_send(3, 0)
    y_near(0, 0)
    x_send(2)
    z_send(1)
    y_near(1, 0)
    z_near(0)
    y_send(0, 3)
    t_step(0)
    y_send(0, 1)
    y_near(2, 0)
    y_near(3, 0)
    y_far(0, 0)
    t_step(1)
    z_near(1)
    y_send(1, 3)
    z_far(0)
    y_far(1, 0)
    x_send(3)
    z_send(2)
    y_near(0, 3)
    y_send(0, 2)
    t_step(2)
    y_near(0, 1)
    y_far(2, 0)
    z_far(1)
    y_send(1, 1)
    y_far(3, 0)
    z_send(3)
    z_near(2)
    y_send(1, 2)
    y_near(1, 3)
    t_pass(0, 0)
    x_send(4)
    z_near(3)
    y_far(0, 3)
    z_far(2)
    y_near(0, 2)
    t_step(3)
    y_far(0, 1)
    y_near(1, 1)
    x_send(5)
    q_pass(0)
    y_send(2, 3)
    z_far(3)
    y_near(1, 2)
    y_far(1, 3)
    y_send(2, 1)
    x_send(6)
    t_pass(1, 0)
    y_send(2, 2)
    t_step(4)
    y_far(0, 2)
    y_send(3, 3)
    b_wait(0)
    y_far(1, 1)
    on(0, (0, 0))
    y_send(3, 1)
    y_near(2, 3)
    y_send(3, 2)
    t_step(5)
    q_pass(1)
    y_far(1, 2)
    y_near(2, 1)
    b_wait(1)
    on(0, (0, 1))
    y_near(2, 2)
    t_step(6)
    t_last()
    on(1, (0, 0))
    q_mid()
    on(0, (1, 0, 0))
    y_far(2, 3)
    y_near(3, 3)
    y_near(3, 1)
    y_near(3, 2)
    on(1, (1, 0))
    on(0, (1, 1, 0))
    q_last()
    on(0, (1, 0, 1))
    y_far(2, 1)
    y_far(2, 2)
    on(0, (1, 1, 1))
    y_far(3, 3)
    y_far(3, 1)
    y_far(3, 2)
    on(1, (0, 1))
    b_wait(2)
    on(0, (0, 2))
    on(1, (1, 1))
    b_wait(3)
    on(0, (1, 2, 0), (1, 2, 1), (1, 3, 0), (1, 3, 1))
    on(1, (0, 2), (1, 2), (1, 3))
    unit(0, 3)
    peak_out(0)
    peak_out(1)

    s1_each(s1_sent)
    for q in range(8 - ND):
        t_send(q).wait_send()

    @pl.when(c == 1)
    def _():
        for q in range(8 - NQ):
            relay(q).wait_send()
        for slot in range(2):
            for q in range(ND):
                t_copy(slot, q).wait_send()

    @pl.when(c == 0)
    def _():
        for q in range(NQ):
            opp_copy(q).wait_send()

    for g in range(G):
        for d in range(2):
            z_copy(g, d).wait_send()
            z_relay(g, d).wait_send()
            for r in rels:
                y_copy(g, r, d).wait_send()
                y_relay(g, r, d).wait_send()
        for r in rels:
            b_copy(g, r, c).wait_send()

    for i in range(8):
        ref = precv.at[i]
        rc(ref, ref, p_ss.at[0], p_rs.at[i], sib).wait_recv()
    top = precv[0]
    for i in range(1, 8):
        top = jnp.maximum(top, precv[i])
    top_ref[...] = top + 1e-06
    for p in range(2):
        for g in range(G):
            ref = orecv.at[:, pl.ds(p * PIECE + START[g], WIDTH[g])]
            rc(ref, ref, o_ss.at[0], o_rs.at[p * G + g], sib).wait_recv()

    for slot in range(2):
        for g in range(G):
            out_move(slot, g, True)
        peak_move(slot, True)


def rescale(hidden_ref, top_ref, all_ref, out_ref, scale_ref):
    for r in range(0, BLOCK, ROWS):
        rows = pl.ds(r, ROWS)
        inv = jnp.broadcast_to(1.0 / top_ref[:1, r:r + ROWS], (ROWS, ROWS)).T
        for k in range(0, NCOL, 128):
            cols = pl.ds(k, 128)
            out_ref[rows, cols] = (hidden_ref[rows, cols].astype(jnp.float32) * inv).astype(jnp.bfloat16)

    @pl.when(pl.program_id(0) == 0)
    def _():
        scale_ref[...] = all_ref[0, :TOK]


def shards(tokens, norm_gain, gate_weight, up_weight):
    dma = pltpu.SemaphoreType.DMA
    vmem = pl.BlockSpec(memory_space=pltpu.VMEM)
    hbm = pl.BlockSpec(memory_space=pl.ANY)
    hidden, tops = pl.pallas_call(
        kernel,
        name="block",
        out_shape=(jax.ShapeDtypeStruct((PAD, NCOL), jnp.bfloat16),
                   jax.ShapeDtypeStruct((8, PAD), jnp.float32)),
        in_specs=[hbm, vmem, hbm, hbm],
        out_specs=(hbm, vmem),
        scratch_shapes=[
            pltpu.VMEM((TOK, D), jnp.bfloat16),
            pltpu.VMEM((3, PAD, D), jnp.bfloat16),
            *[pltpu.VMEM((16, 2, 128, 2 * n), jnp.bfloat16) for n in WIDTH],
            pltpu.VMEM((2, PAD, 128), jnp.float32),
            pltpu.VMEM((2, PAD, PIECE), jnp.bfloat16),
            pltpu.VMEM((2, 8, PAD), jnp.float32),
            pltpu.VMEM((8, 8, PAD), jnp.float32),
            dma, dma((G * 4,)), dma((G * 4,)), dma((8,)), dma((16,)), dma((4,)), dma((8,)), dma((8,)),
            dma((4,)), dma((G * 4,)), dma((G * 4,)), dma((G * 16,)), dma((G * 16,)),
            dma((G * 4,)), dma((G * 4,)), dma((2 * G,)), dma((2 * G,)), dma((8,)), dma((8,)),
        ],
        compiler_params=pltpu.CompilerParams(
            collective_id=0, has_side_effects=True, vmem_limit_bytes=58 * 2**20),
    )(tokens, norm_gain, gate_weight, up_weight)
    return pl.pallas_call(
        rescale,
        name="rescale",
        grid=(PAD // BLOCK,),
        out_shape=(jax.ShapeDtypeStruct((TOK, NCOL), jnp.bfloat16),
                   jax.ShapeDtypeStruct((TOK,), jnp.float32)),
        in_specs=[pl.BlockSpec((BLOCK, NCOL), lambda i: (i, 0)),
                  pl.BlockSpec((8, BLOCK), lambda i: (0, i)),
                  pl.BlockSpec((8, PAD), lambda i: (0, 0))],
        out_specs=(pl.BlockSpec((BLOCK, NCOL), lambda i: (i, 0)),
                   pl.BlockSpec((TOK,), lambda i: (0,))),
    )(hidden, tops, tops)


def solution(mesh):
    in_specs = (P("seq", None), P(), P("seq", "tp"), P("seq", "tp"))
    out_specs = (P("seq", "tp"), P("seq"))
    return jax.shard_map(shards, mesh=mesh, in_specs=in_specs, out_specs=out_specs, check_vma=False)
```
